512 devices in a mesh: prow: 16 (over z, core), pcol: 32 (over x, y).
Axes of the slice: x: 4, y: 8, z: 8, core: 2. Of those that a mesh axis runs over, the one named last changes fastest.
Arguments:
- right_side: bfloat16 [15, 2048, 640], P(None, 'pcol', 'prow'), may hold values from -6 to 6
- lower_panels: bfloat16 [34, 2048, 2048], P(None, 'pcol', 'prow'), may hold values from -0.09375 to 0.09375
- lower_pattern: int32 [34, 32, 32], P(None, 'pcol', 'prow'), may hold values 0 or 1
- upper_panels: bfloat16 [34, 2048, 2048], P(None, 'pcol', 'prow'), may hold values from -0.09375 to 0.09375
- upper_pattern: int32 [34, 32, 32], P(None, 'pcol', 'prow'), may hold values 0 or 1
- lower_inverse: bfloat16 [15, 2048, 2048], P(None, 'pcol', 'prow'), may hold values from -0.2 to 1.2, as said below
- upper_inverse: bfloat16 [15, 2048, 2048], P(None, 'pcol', 'prow'), may hold values from -0.2 to 1.2, as said below
Outputs:
- solution: bfloat16 [15, 2048, 640], P(None, 'pcol', 'prow')
The draws below stay inside these ranges and needn't reach their ends.
Inputs may be any that keep to these rules, and one draw needn't show every extreme that they name: `lower_pattern`: 1 where a block of a panel is nonzero, 0 where it is empty. `upper_pattern`: 1 where a block of a panel is nonzero, 0 where it is empty. `lower_inverse`: the transpose of the given inverse of the diagonal block of each supernode of L. `upper_inverse`: the given inverse of the diagonal block of each supernode of U.
All inputs are finite; a program needn't handle non-finite values.
Results may differ from the reference program's by a relative error of at most 0.04.
Values may be sent and summed in bfloat16 or wider, within the bound.
No kernel may reach another device: no remote copies, remote signals or barrier semaphores. Data moves between devices by JAX's collectives and lax.ppermute only.
A program may use at most 64 MiB of HBM per device.

```python
import jax
import jax.numpy as jnp
from jax import lax

WIDTH = 2048
RHS = 640
NODES = 15
PAIRS = 34
PATTERN_BLOCKS = 32
N_PROW = 16
N_PCOL = 32


def near_identity(key, spread):
    rows = lax.broadcasted_iota(jnp.int32, (NODES, WIDTH, WIDTH), 1)
    cols = lax.broadcasted_iota(jnp.int32, (NODES, WIDTH, WIDTH), 2)
    diagonal = jnp.where(rows == cols, 1.0, 0.0).astype(jnp.float32)
    noise = jax.random.truncated_normal(key, -3.0, 3.0, (NODES, WIDTH, WIDTH), jnp.float32)
    return (diagonal + spread * noise / jnp.sqrt(jnp.float32(WIDTH))).astype(jnp.bfloat16)


def draw_lower_inverse(key, part):
    key = jax.random.fold_in(key, 11)
    return near_identity(key, 0.5)


def draw_upper_inverse(key, part):
    key = jax.random.fold_in(key, 23)
    return near_identity(key, 0.5)


def place_ends(entries, key, low, largest):
    place = [jax.random.randint(jax.random.fold_in(key, axis), (), 0, length) for axis, length in enumerate(entries.shape)]
    widest = entries.shape.index(max(entries.shape))
    beside = place[:widest] + [(place[widest] + 1) % entries.shape[widest]] + place[widest + 1:]
    return entries.at[tuple(place)].set(low).at[tuple(beside)].set(largest)


def levels(stream_key, shape, shards, least, high):
    gain = 1.0
    for position, parts in shards:
        heights = jax.random.uniform(jax.random.fold_in(jax.random.fold_in(stream_key, 6), position), (parts,), jnp.float32, least / len(shards), high / len(shards))
        gain = gain * jnp.repeat(jnp.exp(heights), shape[position] // parts).reshape((-1,) + (1,) * (len(shape) - 1 - position))
    return gain


def centred(stream_key, extent, width, reach, shards=(), kind=jnp.bfloat16):
    drawn = jax.random.normal(stream_key, extent, jnp.float32) * width
    if len(shards) > 0:
        drawn = levels(stream_key, extent, shards, -0.22, 0.18) * drawn
    return jnp.clip(drawn, min=-reach, max=reach).astype(kind)


def setup_inputs(seed: int = 0) -> dict:
    streams_of = jax.random.split(jax.random.key(seed), 8)
    right_side = centred(streams_of[0], (NODES, WIDTH, RHS), 1.0, 6.0, ((1, 32), (2, 16)))
    lower_panels = centred(streams_of[1], (PAIRS, WIDTH, WIDTH), (2 * WIDTH) ** -0.5, 0.09375, ((1, 32), (2, 16)))
    lower_pattern = place_ends((jax.random.randint(streams_of[2], (PAIRS, PATTERN_BLOCKS, PATTERN_BLOCKS), 0, 2) < 1).astype(jnp.int32), jax.random.fold_in(streams_of[2], 1), 0, 1)
    upper_panels = centred(streams_of[3], (PAIRS, WIDTH, WIDTH), (2 * WIDTH) ** -0.5, 0.09375, ((1, 32), (2, 16)))
    upper_pattern = place_ends((jax.random.randint(streams_of[4], (PAIRS, PATTERN_BLOCKS, PATTERN_BLOCKS), 0, 2) < 1).astype(jnp.int32), jax.random.fold_in(streams_of[4], 1), 0, 1)
    lower_inverse = draw_lower_inverse(jax.random.fold_in(streams_of[7], 71), 0)
    upper_inverse = draw_upper_inverse(jax.random.fold_in(streams_of[7], 71), 0)
    return dict(right_side=right_side, lower_panels=lower_panels, lower_pattern=lower_pattern, upper_panels=upper_panels, upper_pattern=upper_pattern, lower_inverse=lower_inverse, upper_inverse=upper_inverse)


node_offsets = (0, 8, 12, 14)


def pair_offset(desc_level, anc_level):
    offset = 0
    for first_level in range(4):
        for second_level in range(first_level + 1, 4):
            if first_level == desc_level and second_level == anc_level:
                return offset
            offset = offset + 2 ** (3 - first_level)
    return offset


def bf16_round(values):
    rounded = values.astype(jnp.bfloat16)
    rounded = lax.optimization_barrier(rounded)
    return rounded.astype(jnp.float32)


def split_sum(products, pieces, out_shape):
    def add_piece(piece_index, summed):
        running = jnp.zeros(out_shape, jnp.float32)
        for panels, pattern, vectors, fanout, gathering in products:
            piece_cols = panels.shape[2] // pieces
            first_col = (piece_index * piece_cols).astype(jnp.int32)
            block_cols = lax.dynamic_slice_in_dim(panels, first_col, piece_cols, 2).astype(jnp.float32)
            if pattern is not None:
                block_span = pattern.shape[2] // pieces
                first_block = (piece_index * block_span).astype(jnp.int32)
                kept_blocks = lax.dynamic_slice_in_dim(pattern, first_block, block_span, 2)
                row_size = panels.shape[1] // pattern.shape[1]
                col_size = piece_cols // block_span
                shaped = block_cols.reshape(panels.shape[0], pattern.shape[1], row_size, block_span, col_size)
                shaped = jnp.where(kept_blocks[:, :, None, :, None] > 0, shaped, jnp.zeros((), jnp.float32))
                block_cols = shaped.reshape(panels.shape[0], panels.shape[1], piece_cols)
            vec_rows = lax.dynamic_slice_in_dim(vectors, first_col, piece_cols, 1).astype(jnp.float32)
            group_count = panels.shape[0] // fanout
            grouped = block_cols.reshape(group_count, fanout, panels.shape[1], piece_cols)
            if gathering:
                stacked = vec_rows.reshape(group_count, fanout, piece_cols, vec_rows.shape[2])
                running = running + jnp.einsum("gfab,gfbr->gar", grouped, stacked)
            else:
                spread = jnp.einsum("gfab,gbr->gfar", grouped, vec_rows)
                running = running + spread.reshape(out_shape)
        return summed + bf16_round(running)

    return lax.fori_loop(0, pieces, add_piece, jnp.zeros(out_shape, jnp.float32))


def reference(right_side, lower_panels, lower_pattern, upper_panels, upper_pattern, lower_inverse, upper_inverse):
    upper_panels = jnp.swapaxes(upper_panels, 1, 2)
    upper_pattern = jnp.swapaxes(upper_pattern, 1, 2)
    lower_inverse = jnp.swapaxes(lower_inverse, 1, 2)
    columns = right_side.shape[2]
    order = right_side.shape[1]
    forward = []
    for height in range(4):
        offset = node_offsets[height]
        amount = 2 ** (3 - height)
        source = right_side[offset:offset + amount]
        if height > 0:
            products = []
            for desc_level in range(height):
                pair_first = pair_offset(desc_level, height)
                fanout = 2 ** (height - desc_level)
                group_size = 2 ** (3 - desc_level)
                products.append((lower_panels[pair_first:pair_first + group_size],
                                 lower_pattern[pair_first:pair_first + group_size],
                                 forward[desc_level], fanout, True))
            update = split_sum(products, N_PROW, (amount, order, columns))
            residual = (source.astype(jnp.float32) - update).astype(jnp.bfloat16)
        else:
            residual = source
        inverse = lower_inverse[offset:offset + amount]
        solved = split_sum([(inverse, None, residual, 1, True)], N_PCOL, (amount, order, columns))
        forward.append(solved.astype(jnp.bfloat16))
    backward = [None, None, None, None]
    for height in (3, 2, 1, 0):
        offset = node_offsets[height]
        amount = 2 ** (3 - height)
        if height < 3:
            products = []
            for anc_level in range(height + 1, 4):
                pair_first = pair_offset(height, anc_level)
                fanout = 2 ** (anc_level - height)
                products.append((upper_panels[pair_first:pair_first + amount],
                                 upper_pattern[pair_first:pair_first + amount],
                                 backward[anc_level], fanout, False))
            update = split_sum(products, N_PCOL, (amount, order, columns))
            residual = (forward[height].astype(jnp.float32) - update).astype(jnp.bfloat16)
        else:
            residual = forward[height]
        inverse = upper_inverse[offset:offset + amount]
        solved = split_sum([(inverse, None, residual, 1, True)], N_PROW, (amount, order, columns))
        backward[height] = solved.astype(jnp.bfloat16)
    return jnp.concatenate(backward, axis=0)
```

```python
import jax
import jax.numpy as jnp
from jax import lax
from jax.sharding import Mesh, PartitionSpec as P

BF = jnp.bfloat16
F32 = jnp.float32
PROW = ("z", "core")
Y = ("y2", "y1", "y0")
YHIGH = ("y2", "y1")
GROUP = ("x", "y0")


def swap(blocks, axes):
    return lax.all_to_all(blocks, axes, 0, 0, tiled=True)


def share(block, axes, count):
    return swap(jnp.broadcast_to(block[None], (count,) + block.shape), axes)


def masked(panels, pattern):
    lane = lax.broadcasted_iota(jnp.int32, (1, 1, panels.shape[2]), 2)
    keep = jnp.where(lane < panels.shape[2] // 2, pattern[:, :, 0:1], pattern[:, :, 1:2])
    return jnp.where(keep > 0, panels, jnp.zeros((), panels.dtype))


def spread_leaf(tiles):
    return jnp.swapaxes(swap(jnp.stack(tiles, axis=1), Y), 0, 1)


def spread_upper(tiles):
    wide = [jnp.repeat(t, 4 // t.shape[0], axis=0) for t in tiles]
    return jnp.swapaxes(swap(jnp.stack(wide, axis=1), YHIGH), 0, 1)


def gather(parts):
    flat = jnp.concatenate([p.reshape((-1,) + p.shape[2:]) for p in parts], axis=0)
    full = lax.all_gather(flat, PROW, axis=0, tiled=False)
    out, at = [], 0
    for p in parts:
        got = []
        for _ in range(p.shape[0]):
            got.append(full[:, at : at + p.shape[1]])
            at += p.shape[1]
        out.append(got)
    return out


def by_rows(panel, vector):
    return jnp.einsum("pnc,psrc->snr", vector, panel, preferred_element_type=F32)


def by_cols(panel, vector):
    return jnp.einsum("snr,psrc->pnc", vector, panel, preferred_element_type=F32)


def sum_x(part):
    return share(part.astype(BF), "x", 4).astype(F32).reshape((4,) + part.shape).sum(0)


def scatter_group(part):
    pieces = swap(part.astype(BF).reshape(8, 2, *part.shape[1:]), GROUP)
    return pieces.astype(F32).sum(0)


def gather_group(own):
    return share(own, GROUP, 8).reshape((16,) + own.shape[1:])


def local(right_side, lower_panels, lower_pattern, upper_panels, upper_pattern, lower_inverse, upper_inverse):
    y0 = lax.axis_index("y0")
    y1 = lax.axis_index("y1")
    yi = lax.axis_index(Y)
    gi = lax.axis_index(GROUP)

    low = masked(lower_panels, lower_pattern)
    up = masked(upper_panels, upper_pattern)
    li, ui = lower_inverse, upper_inverse

    rhs = jnp.swapaxes(right_side, 1, 2)
    nodes = jnp.stack(
        [rhs[0:8], jnp.repeat(rhs[8:12], 2, 0), jnp.repeat(rhs[12:14], 4, 0), jnp.repeat(rhs[14:15], 8, 0)], axis=1
    )
    nodes = swap(nodes, Y)
    b0 = nodes[:, 0]
    n = b0.shape[1]
    upper_b = nodes[:, 1:].reshape(4, 2, 3, n, 64)
    upper_b = jnp.where(y0 == 0, upper_b[:, 0], upper_b[:, 1]).astype(F32)

    (p_li0, p_l01), = gather([spread_leaf([li[0:8], low[0:8]])])
    upper_fwd = spread_upper([li[8:12], low[24:28], low[28:32], li[12:14], low[32:34], li[14:15]])
    leaf_fwd = spread_leaf([low[8:16], low[16:24]])
    (p_l02, p_l03), (p_li1, p_l12, p_l13, p_li2, p_l23, p_li3) = gather([leaf_fwd, upper_fwd])
    upper_bwd = spread_upper([ui[14:15], up[32:34], ui[12:14], up[24:28], up[28:32], ui[8:12]])
    leaf_bwd = spread_leaf([up[0:8], up[8:16], up[16:24], ui[0:8]])
    (p_ui3, p_u23, p_ui2, p_u12, p_u13, p_ui1), (p_u01, p_u02, p_u03, p_ui0) = gather([upper_bwd, leaf_bwd])

    def parity(blocks):
        return jnp.swapaxes(blocks.reshape((4, 2) + blocks.shape[1:]), 0, 1)

    mine = (lax.broadcasted_iota(jnp.int32, (2, 1, 1, 1), 0) == y0)

    def add_mine(blocks, extra):
        return blocks + jnp.where(mine, extra[None], 0.0)

    v0 = sum_x(by_cols(p_li0, b0)).astype(BF)
    part = parity(by_rows(p_l01, v0)).astype(BF)
    update = swap(part, "y0").astype(F32).sum(0)
    res = (upper_b[:, 0] - update).astype(BF)

    own1 = scatter_group(by_cols(p_li1, res)).astype(BF)
    v1 = gather_group(own1)
    part = add_mine(parity(by_rows(p_l02, v0)), by_rows(p_l12, v1)).astype(BF)
    part = jnp.broadcast_to(part[None], (2,) + part.shape).reshape((4,) + part.shape[1:])
    update = swap(part, ("y1", "y0")).astype(F32).sum(0)
    res = (upper_b[:, 1] - update).astype(BF)

    own2 = scatter_group(by_cols(p_li2, res)).astype(BF)
    v2 = gather_group(own2)
    top = by_rows(p_l13, v1) + jnp.where(y1 == 0, by_rows(p_l23, v2), 0.0)
    part = add_mine(parity(by_rows(p_l03, v0)), top).astype(BF)
    part = jnp.broadcast_to(part[None], (4,) + part.shape).reshape((8,) + part.shape[1:])
    update = swap(part, Y).astype(F32).sum(0)
    res = (upper_b[:, 2] - update).astype(BF)

    v3 = gather_group(scatter_group(by_cols(p_li3, res)).astype(BF))

    s3 = by_rows(p_ui3, v3).astype(BF)
    own = own2.astype(F32) - scatter_group(by_cols(p_u23, s3))
    s2 = by_rows(p_ui2, gather_group(own.astype(BF))).astype(BF)
    own = own1.astype(F32) - scatter_group(by_cols(p_u12, s2) + by_cols(p_u13, s3))
    s1 = by_rows(p_ui1, gather_group(own.astype(BF))).astype(BF)

    uppers = share(jnp.stack([s1, s2, s3]), "y0", 2).reshape(2, 3, 4, n, 64)
    uppers = jnp.transpose(uppers, (1, 2, 0, 3, 4)).reshape(3, 8, n, 64)
    part = by_cols(p_u01, uppers[0]) + by_cols(p_u02, uppers[1]) + by_cols(p_u03, uppers[2])
    res = (v0.astype(F32) - sum_x(part)).astype(BF)
    s0 = by_rows(p_ui0, res).astype(BF)

    got = swap(jnp.stack([s0, uppers[0], uppers[1]], axis=1), Y)
    last = lax.dynamic_index_in_dim(uppers[2], yi, 0, keepdims=True)
    out = jnp.concatenate([got[:, 0], got[0::2, 1], got[0::4, 2], last], axis=0)
    return jnp.swapaxes(out, 1, 2)


def solution(mesh):
    fine = Mesh(mesh.devices.reshape(8, 2, 4, 2, 2, 2), ("z", "core", "x", "y2", "y1", "y0"))
    spec = P(None, ("x", "y2", "y1", "y0"), ("z", "core"))
    return jax.shard_map(local, mesh=fine, in_specs=(spec,) * 7, out_specs=spec, check_vma=False)
```

```python
import jax
import jax.numpy as jnp
from jax import lax
from jax.sharding import Mesh, PartitionSpec as P

BF = jnp.bfloat16
F32 = jnp.float32
PROW = ("z", "core")
Y = ("y2", "y1", "y0")
YHIGH = ("y2", "y1")


def swap(blocks, axes):
    return lax.all_to_all(blocks, axes, 0, 0, tiled=True)


def share(block, axes, count):
    return swap(jnp.broadcast_to(block[None], (count,) + block.shape), axes)


def masked(panels, pattern):
    lane = lax.broadcasted_iota(jnp.int32, (1, 1, panels.shape[2]), 2)
    keep = jnp.where(lane < panels.shape[2] // 2, pattern[:, :, 0:1], pattern[:, :, 1:2])
    return jnp.where(keep > 0, panels, jnp.zeros((), panels.dtype))


def spread_leaf(tiles):
    return jnp.swapaxes(swap(jnp.stack(tiles, axis=1), Y), 0, 1)


def spread_upper(tiles):
    wide = [jnp.repeat(t, 4 // t.shape[0], axis=0) for t in tiles]
    return jnp.swapaxes(swap(jnp.stack(wide, axis=1), YHIGH), 0, 1)


def gather(parts, groups=None):
    flat = jnp.concatenate([p.reshape((-1,) + p.shape[2:]) for p in parts], axis=0)
    full = lax.all_gather(flat, PROW, axis=0, tiled=False)
    out, at = [], 0
    for p, sizes in zip(parts, groups):
        got = []
        for size in sizes:
            got.append(full[:, at : at + size * p.shape[1]])
            at += size * p.shape[1]
        out.append(got)
    return out


def collect(part, axis):
    return lax.all_gather(part, axis, axis=0, tiled=False).astype(F32).sum(0)


def by_rows(panel, vector):
    return jnp.einsum("pnc,psrc->snr", vector, panel, preferred_element_type=F32)


def by_cols(panel, vector):
    return jnp.einsum("snr,psrc->pnc", vector, panel, preferred_element_type=F32)


def sum_x(part):
    return share(part.astype(BF), "x", 4).astype(F32).reshape((4,) + part.shape).sum(0)


def local(right_side, lower_panels, lower_pattern, upper_panels, upper_pattern, lower_inverse, upper_inverse):
    y0 = lax.axis_index("y0")
    yi = lax.axis_index(Y)

    li, ui = lower_inverse, upper_inverse
    head = masked(lower_panels[0:8], lower_pattern[0:8])

    def parity(blocks):
        pairs = blocks.reshape(blocks.shape[:-3] + (4, 2) + blocks.shape[-2:])
        return jnp.where(y0 == 0, pairs[..., 0, :, :], pairs[..., 1, :, :])

    first = spread_leaf([li[0:8], head, jnp.repeat(li[8:12], 2, 0)])
    (p_li0, p_l01), (p_li1,) = gather([first[0:2], parity(first[2:3])], ((1, 1), (1,)))

    right_side, lower_panels, lower_pattern, li, first = lax.optimization_barrier(
        (right_side, lower_panels, lower_pattern, li, first)
    )
    low = masked(lower_panels, lower_pattern)
    rhs = jnp.swapaxes(right_side, 1, 2)
    nodes = jnp.stack(
        [rhs[0:8], jnp.repeat(rhs[8:12], 2, 0), jnp.repeat(rhs[12:14], 4, 0), jnp.repeat(rhs[14:15], 8, 0)], axis=1
    )
    nodes = swap(nodes, Y)
    b0 = nodes[:, 0]
    n = b0.shape[1]
    b1, b2, b3 = (nodes[:, k].astype(F32) for k in (1, 2, 3))

    leaf_fwd = spread_leaf([low[8:16], low[16:24], jnp.repeat(li[12:14], 4, 0), jnp.repeat(li[14:15], 8, 0)])
    upper_fwd = spread_upper([low[24:28], low[28:32], low[32:34]])
    p_leaf, p_upper = gather([leaf_fwd, upper_fwd], ((2, 1, 1), (2, 1)))
    (p_l0, p_li2, p_li3), (p_l1, p_l23) = p_leaf, p_upper

    mine = lax.broadcasted_iota(jnp.int32, (1, 1, 2, 1, 1), 2) == y0

    nothing = (leaf_fwd[0, 0, 0, 0] + upper_fwd[0, 0, 0, 0]) * jnp.zeros((), BF)
    part = by_cols(p_li0, b0 + nothing).astype(BF)
    part, upper_panels, upper_pattern, ui = lax.optimization_barrier((part, upper_panels, upper_pattern, ui))
    up = masked(upper_panels, upper_pattern)
    upper_bwd = spread_upper([ui[14:15], up[32:34], ui[12:14], up[24:28], up[28:32], ui[8:12]])
    v0 = collect(part, "x").astype(BF)

    v0, up, ui, upper_bwd = lax.optimization_barrier((v0, up, ui, upper_bwd))
    (p_ui3, p_u23, p_ui2, p_u1, p_ui1), = gather([upper_bwd], ((1, 1, 1, 2, 1),))
    leaf_bwd = spread_leaf([up[0:8], up[8:16], up[16:24], ui[0:8]])
    update = parity(collect(by_rows(p_l01, v0).astype(BF), "y0"))
    part = by_cols(p_li1, (parity(b1) - update).astype(BF)).astype(BF)
    v1 = collect(part, "x").astype(BF)
    v1, leaf_bwd = lax.optimization_barrier((v1, leaf_bwd))
    (p_u0, p_ui0), = gather([leaf_bwd], ((3, 1),))
    v1 = lax.optimization_barrier(collect(v1, "y0").astype(BF))

    leaf_part = by_rows(p_l0, v0).reshape(2, 4, 2, n, 64)
    node_part = by_rows(p_l1, v1).reshape(2, 4, 1, n, 64)
    part = (leaf_part + jnp.where(mine, node_part, 0.0)).astype(BF).reshape(2, 8, n, 64)
    quad = share(part, ("y1", "y0"), 4).astype(F32).reshape(4, 2, 8, n, 64).sum(0)
    v2 = sum_x(by_cols(p_li2, (b2 - quad[0]).astype(BF))).astype(BF)

    part = (parity(quad[1]) + by_rows(p_l23, v2)).astype(BF)
    update = share(part, ("y2", "y0"), 4).astype(F32).reshape(2, 2, 4, n, 64).sum(0)
    update = jnp.swapaxes(update, 0, 1).reshape(8, n, 64)
    v3 = sum_x(by_cols(p_li3, (b3 - update).astype(BF))).astype(BF)

    def collect_group(part):
        return collect(collect(part.astype(BF), "x").astype(BF), "y0")

    s3 = by_rows(p_ui3, v3).astype(BF)
    res = v2.astype(F32) - collect_group(by_cols(p_u23, s3))
    s2 = by_rows(p_ui2, res.astype(BF)).astype(BF)
    res = v1.astype(F32) - collect_group(by_cols(p_u1, jnp.concatenate([s2, s3], axis=0)))
    s1 = by_rows(p_ui1, res.astype(BF)).astype(BF)

    uppers = lax.all_gather(jnp.stack([s1, s2, s3]), "y0", axis=0, tiled=False)
    uppers = jnp.transpose(uppers, (1, 2, 0, 3, 4)).reshape(3, 8, n, 64)
    part = by_cols(p_u0, uppers.reshape(24, n, 64))
    res = (v0.astype(F32) - sum_x(part)).astype(BF)
    s0 = by_rows(p_ui0, res).astype(BF)

    got = swap(jnp.stack([s0, uppers[0], uppers[1]], axis=1), Y)
    last = lax.dynamic_index_in_dim(uppers[2], yi, 0, keepdims=True)
    out = jnp.concatenate([got[:, 0], got[0::2, 1], got[0::4, 2], last], axis=0)
    return jnp.swapaxes(out, 1, 2)


def solution(mesh):
    fine = Mesh(mesh.devices.reshape(8, 2, 4, 2, 2, 2), ("z", "core", "x", "y2", "y1", "y0"))
    spec = P(None, ("x", "y2", "y1", "y0"), ("z", "core"))
    return jax.shard_map(local, mesh=fine, in_specs=(spec,) * 7, out_specs=spec, check_vma=False)
```

```python
import jax
import jax.numpy as jnp
from jax import lax
from jax.sharding import Mesh, PartitionSpec as P

BF = jnp.bfloat16
F32 = jnp.float32
PROW = ("z", "core")
Y = ("y2", "y1", "y0")
YHIGH = ("y2", "y1")


def swap(blocks, axes):
    return lax.all_to_all(blocks, axes, 0, 0, tiled=True)


def share(block, axes, count):
    return swap(jnp.broadcast_to(block[None], (count,) + block.shape), axes)


def masked(panels, pattern):
    lane = lax.broadcasted_iota(jnp.int32, (1, 1, panels.shape[2]), 2)
    keep = jnp.where(lane < panels.shape[2] // 2, pattern[:, :, 0:1], pattern[:, :, 1:2])
    return jnp.where(keep > 0, panels, jnp.zeros((), panels.dtype))


def spread_leaf(tiles):
    return jnp.swapaxes(swap(jnp.stack(tiles, axis=1), Y), 0, 1)


def spread_upper(tiles):
    wide = [jnp.repeat(t, 4 // t.shape[0], axis=0) for t in tiles]
    return jnp.swapaxes(swap(jnp.stack(wide, axis=1), YHIGH), 0, 1)


def gather(parts, groups=None):
    flat = jnp.concatenate([p.reshape((-1,) + p.shape[2:]) for p in parts], axis=0)
    full = lax.all_gather(flat, PROW, axis=0, tiled=False)
    out, at = [], 0
    for p, sizes in zip(parts, groups):
        got = []
        for size in sizes:
            got.append(full[:, at : at + size * p.shape[1]])
            at += size * p.shape[1]
        out.append(got)
    return out


def collect(part, axis):
    return lax.all_gather(part, axis, axis=0, tiled=False).astype(F32).sum(0)


def by_rows(panel, vector):
    return jnp.einsum("pnc,psrc->snr", vector, panel, preferred_element_type=F32)


def by_cols(panel, vector):
    return jnp.einsum("snr,psrc->pnc", vector, panel, preferred_element_type=F32)


def sum_x(part):
    return share(part.astype(BF), "x", 4).astype(F32).reshape((4,) + part.shape).sum(0)


def local(right_side, lower_panels, lower_pattern, upper_panels, upper_pattern, lower_inverse, upper_inverse):
    y0 = lax.axis_index("y0")
    yi = lax.axis_index(Y)

    li, ui = lower_inverse, upper_inverse
    head = masked(lower_panels[0:8], lower_pattern[0:8])

    def parity(blocks):
        pairs = blocks.reshape(blocks.shape[:-3] + (4, 2) + blocks.shape[-2:])
        return jnp.where(y0 == 0, pairs[..., 0, :, :], pairs[..., 1, :, :])

    first = spread_leaf([li[0:8], head, jnp.repeat(li[8:12], 2, 0)])
    (p_li0, p_l01), (p_li1,) = gather([first[0:2], parity(first[2:3])], ((1, 1), (1,)))

    right_side, lower_panels, lower_pattern, li, first = lax.optimization_barrier(
        (right_side, lower_panels, lower_pattern, li, first)
    )
    low = masked(lower_panels, lower_pattern)
    rhs = jnp.swapaxes(right_side, 1, 2)
    nodes = jnp.stack(
        [rhs[0:8], jnp.repeat(rhs[8:12], 2, 0), jnp.repeat(rhs[12:14], 4, 0), jnp.repeat(rhs[14:15], 8, 0)], axis=1
    )
    nodes = swap(nodes, Y)
    b0 = nodes[:, 0]
    n = b0.shape[1]
    b1, b2, b3 = (nodes[:, k].astype(F32) for k in (1, 2, 3))

    leaf_fwd = spread_leaf([low[8:16], low[16:24], jnp.repeat(li[12:14], 4, 0), jnp.repeat(li[14:15], 8, 0),
                            jnp.repeat(ui[8:12], 2, 0)])
    upper_fwd = spread_upper([low[24:28], low[28:32], low[32:34]])
    p_leaf, p_upper = gather([leaf_fwd[0:4], upper_fwd], ((2, 1, 1), (2, 1)))
    (p_l0, p_li2, p_li3), (p_l1, p_l23) = p_leaf, p_upper

    mine = lax.broadcasted_iota(jnp.int32, (1, 1, 2, 1, 1), 2) == y0

    nothing = (leaf_fwd[0, 0, 0, 0] + upper_fwd[0, 0, 0, 0]) * jnp.zeros((), BF)
    part = by_cols(p_li0, b0 + nothing).astype(BF)
    part, upper_panels, upper_pattern, ui = lax.optimization_barrier((part, upper_panels, upper_pattern, ui))
    up = masked(upper_panels, upper_pattern)
    upper_bwd = spread_upper([ui[14:15], up[32:34], ui[12:14], up[24:28], up[28:32]])
    v0 = collect(part, "x").astype(BF)

    v0, up, ui, upper_bwd = lax.optimization_barrier((v0, up, ui, upper_bwd))
    (p_ui1,), (p_ui3, p_u23, p_ui2, p_u1) = gather([leaf_fwd[4:5], upper_bwd], ((1,), (1, 1, 1, 2)))
    leaf_bwd = spread_leaf([up[0:8], up[8:16], up[16:24], ui[0:8]])
    update = parity(collect(by_rows(p_l01, v0).astype(BF), "y0"))
    part = by_cols(p_li1, (parity(b1) - update).astype(BF)).astype(BF)
    v1 = collect(part, "x").astype(BF)
    v1, leaf_bwd = lax.optimization_barrier((v1, leaf_bwd))
    (p_u0, p_ui0), = gather([leaf_bwd], ((3, 1),))
    v1 = lax.optimization_barrier(collect(v1, "y0").astype(BF))

    leaf_part = by_rows(p_l0, v0).reshape(2, 4, 2, n, 64)
    node_part = by_rows(p_l1, v1).reshape(2, 4, 1, n, 64)
    part = (leaf_part + jnp.where(mine, node_part, 0.0)).astype(BF).reshape(2, 8, n, 64)
    quad = share(part, ("y1", "y0"), 4).astype(F32).reshape(4, 2, 8, n, 64).sum(0)
    v2 = sum_x(by_cols(p_li2, (b2 - quad[0]).astype(BF))).astype(BF)

    part = (parity(quad[1]) + by_rows(p_l23, v2)).astype(BF)
    update = share(part, ("y2", "y0"), 4).astype(F32).reshape(2, 2, 4, n, 64).sum(0)
    update = jnp.swapaxes(update, 0, 1).reshape(8, n, 64)
    v3 = sum_x(by_cols(p_li3, (b3 - update).astype(BF))).astype(BF)

    def collect_group(part):
        return collect(collect(part.astype(BF), "x").astype(BF), "y0")

    s3 = by_rows(p_ui3, v3).astype(BF)
    res = v2.astype(F32) - collect_group(by_cols(p_u23, s3))
    s2 = by_rows(p_ui2, res.astype(BF)).astype(BF)
    part = by_cols(p_u1, jnp.concatenate([s2, s3], axis=0)).astype(BF)
    part = share(part, "x", 4).astype(F32).reshape(4, 16, n, 128).sum(0).astype(BF)
    above = lax.all_gather(jnp.stack([s2, s3]), "y0", axis=0, tiled=False)
    above = jnp.transpose(above, (1, 2, 0, 3, 4)).reshape(2, 8, n, 64)
    part, above = lax.optimization_barrier((part, above))
    res = v1.astype(F32) - collect(part, "y0")
    s1 = by_rows(p_ui1, res.astype(BF)).astype(BF)

    uppers = jnp.concatenate([s1[None], above], axis=0)
    part = by_cols(p_u0, uppers.reshape(24, n, 64))
    res = (v0.astype(F32) - sum_x(part)).astype(BF)
    s0 = by_rows(p_ui0, res).astype(BF)

    got = swap(jnp.stack([s0, uppers[0], uppers[1]], axis=1), Y)
    last = lax.dynamic_index_in_dim(uppers[2], yi, 0, keepdims=True)
    out = jnp.concatenate([got[:, 0], got[0::2, 1], got[0::4, 2], last], axis=0)
    return jnp.swapaxes(out, 1, 2)


def solution(mesh):
    fine = Mesh(mesh.devices.reshape(8, 2, 4, 2, 2, 2), ("z", "core", "x", "y2", "y1", "y0"))
    spec = P(None, ("x", "y2", "y1", "y0"), ("z", "core"))
    return jax.shard_map(local, mesh=fine, in_specs=(spec,) * 7, out_specs=spec, check_vma=False)
```

```python
import jax
import jax.numpy as jnp
from jax import lax
from jax.sharding import Mesh, PartitionSpec as P

BF = jnp.bfloat16
F32 = jnp.float32
PROW = ("z", "core")
Y = ("y2", "y1", "y0")
YHIGH = ("y2", "y1")


def swap(blocks, axes):
    return lax.all_to_all(blocks, axes, 0, 0, tiled=True)


def share(block, axes, count):
    return swap(jnp.broadcast_to(block[None], (count,) + block.shape), axes)


def masked(panels, pattern):
    lane = lax.broadcasted_iota(jnp.int32, (1, 1, panels.shape[2]), 2)
    keep = jnp.where(lane < panels.shape[2] // 2, pattern[:, :, 0:1], pattern[:, :, 1:2])
    return jnp.where(keep > 0, panels, jnp.zeros((), panels.dtype))


def spread_leaf(tiles):
    return jnp.swapaxes(swap(jnp.stack(tiles, axis=1), Y), 0, 1)


def spread_upper(tiles):
    wide = [jnp.repeat(t, 4 // t.shape[0], axis=0) for t in tiles]
    return jnp.swapaxes(swap(jnp.stack(wide, axis=1), YHIGH), 0, 1)


def gather(parts, groups=None):
    flat = jnp.concatenate([p.reshape((-1,) + p.shape[2:]) for p in parts], axis=0)
    full = lax.all_gather(flat, PROW, axis=0, tiled=False)
    out, at = [], 0
    for p, sizes in zip(parts, groups):
        got = []
        for size in sizes:
            got.append(full[:, at : at + size * p.shape[1]])
            at += size * p.shape[1]
        out.append(got)
    return out


def collect(part, axis):
    return lax.all_gather(part, axis, axis=0, tiled=False).astype(F32).sum(0)


def by_rows(panel, vector):
    return jnp.einsum("pnc,psrc->snr", vector, panel, preferred_element_type=F32)


def by_cols(panel, vector):
    return jnp.einsum("snr,psrc->pnc", vector, panel, preferred_element_type=F32)


def sum_x(part):
    return share(part.astype(BF), "x", 4).astype(F32).reshape((4,) + part.shape).sum(0)


def local(right_side, lower_panels, lower_pattern, upper_panels, upper_pattern, lower_inverse, upper_inverse):
    y0 = lax.axis_index("y0")
    yi = lax.axis_index(Y)

    li, ui = lower_inverse, upper_inverse
    head = masked(lower_panels[0:8], lower_pattern[0:8])

    def parity(blocks):
        pairs = blocks.reshape(blocks.shape[:-3] + (4, 2) + blocks.shape[-2:])
        return jnp.where(y0 == 0, pairs[..., 0, :, :], pairs[..., 1, :, :])

    first = spread_leaf([li[0:8], head, jnp.repeat(li[8:12], 2, 0)])
    (p_li0, p_l01), (p_li1,) = gather([first[0:2], parity(first[2:3])], ((1, 1), (1,)))

    right_side, lower_panels, lower_pattern, li, first = lax.optimization_barrier(
        (right_side, lower_panels, lower_pattern, li, first)
    )
    low = masked(lower_panels, lower_pattern)
    rhs = jnp.swapaxes(right_side, 1, 2)
    nodes = jnp.stack(
        [rhs[0:8], jnp.repeat(rhs[8:12], 2, 0), jnp.repeat(rhs[12:14], 4, 0), jnp.repeat(rhs[14:15], 8, 0)], axis=1
    )
    nodes = swap(nodes, Y)
    b0 = nodes[:, 0]
    n = b0.shape[1]
    b1, b2, b3 = (nodes[:, k].astype(F32) for k in (1, 2, 3))

    leaf_fwd = spread_leaf([low[8:16], low[16:24], jnp.repeat(li[12:14], 4, 0), jnp.repeat(li[14:15], 8, 0),
                            jnp.repeat(ui[8:12], 2, 0)])
    upper_fwd = spread_upper([low[24:28], low[28:32], low[32:34]])
    p_leaf, p_upper = gather([leaf_fwd[0:4], upper_fwd], ((2, 1, 1), (2, 1)))
    (p_l0, p_li2, p_li3), (p_l1, p_l23) = p_leaf, p_upper

    mine = lax.broadcasted_iota(jnp.int32, (1, 1, 2, 1, 1), 2) == y0

    nothing = (leaf_fwd[0, 0, 0, 0] + upper_fwd[0, 0, 0, 0]) * jnp.zeros((), BF)
    part = by_cols(p_li0, b0 + nothing).astype(BF)
    part, upper_panels, upper_pattern, ui = lax.optimization_barrier((part, upper_panels, upper_pattern, ui))
    up = masked(upper_panels, upper_pattern)
    upper_bwd = spread_upper([ui[14:15], up[32:34], ui[12:14], up[24:28], up[28:32]])
    v0 = collect(part, "x").astype(BF)

    v0, up, ui, upper_bwd = lax.optimization_barrier((v0, up, ui, upper_bwd))
    (p_ui1,), (p_ui3, p_u23, p_ui2, p_u1) = gather([leaf_fwd[4:5], upper_bwd], ((1,), (1, 1, 1, 2)))
    leaf_bwd = spread_leaf([up[0:8], up[8:16], up[16:24], ui[0:8]])
    update = parity(collect(by_rows(p_l01, v0).astype(BF), "y0"))
    part = by_cols(p_li1, (parity(b1) - update).astype(BF)).astype(BF)
    v1 = collect(part, "x").astype(BF)
    v1, leaf_bwd = lax.optimization_barrier((v1, leaf_bwd))
    (p_u0, p_ui0), = gather([leaf_bwd], ((3, 1),))
    v1 = lax.optimization_barrier(collect(v1, "y0").astype(BF))

    leaf_part = by_rows(p_l0, v0).reshape(2, 4, 2, n, 64)
    node_part = by_rows(p_l1, v1).reshape(2, 4, 1, n, 64)
    part = (leaf_part + jnp.where(mine, node_part, 0.0)).astype(BF).reshape(2, 8, n, 64)
    quad = share(part, ("y1", "y0"), 4).astype(F32).reshape(4, 2, 8, n, 64).sum(0)
    v2 = collect(by_cols(p_li2, (b2 - quad[0]).astype(BF)).astype(BF), "x").astype(BF)

    part = (parity(quad[1]) + by_rows(p_l23, v2)).astype(BF)
    update = share(part, ("y2", "y0"), 4).astype(F32).reshape(2, 2, 4, n, 64).sum(0)
    update = jnp.swapaxes(update, 0, 1).reshape(8, n, 64)
    v3 = sum_x(by_cols(p_li3, (b3 - update).astype(BF))).astype(BF)

    def collect_group(part):
        return collect(collect(part.astype(BF), "x").astype(BF), "y0")

    s3 = by_rows(p_ui3, v3).astype(BF)
    res = v2.astype(F32) - collect_group(by_cols(p_u23, s3))
    s2 = by_rows(p_ui2, res.astype(BF)).astype(BF)
    part = by_cols(p_u1, jnp.concatenate([s2, s3], axis=0)).astype(BF)
    part = share(part, "x", 4).astype(F32).reshape(4, 16, n, 128).sum(0).astype(BF)
    above = lax.all_gather(jnp.stack([s2, s3]), "y0", axis=0, tiled=False)
    above = jnp.transpose(above, (1, 2, 0, 3, 4)).reshape(2, 8, n, 64)
    part, above = lax.optimization_barrier((part, above))
    res = v1.astype(F32) - collect(part, "y0")
    s1 = by_rows(p_ui1, res.astype(BF)).astype(BF)

    uppers = jnp.concatenate([s1[None], above], axis=0)
    part = by_cols(p_u0, uppers.reshape(24, n, 64))
    res = (v0.astype(F32) - sum_x(part)).astype(BF)
    s0 = by_rows(p_ui0, res).astype(BF)

    got = swap(jnp.stack([s0, uppers[0], uppers[1]], axis=1), Y)
    last = lax.dynamic_index_in_dim(uppers[2], yi, 0, keepdims=True)
    out = jnp.concatenate([got[:, 0], got[0::2, 1], got[0::4, 2], last], axis=0)
    return jnp.swapaxes(out, 1, 2)


def solution(mesh):
    fine = Mesh(mesh.devices.reshape(8, 2, 4, 2, 2, 2), ("z", "core", "x", "y2", "y1", "y0"))
    spec = P(None, ("x", "y2", "y1", "y0"), ("z", "core"))
    return jax.shard_map(local, mesh=fine, in_specs=(spec,) * 7, out_specs=spec, check_vma=False)
```
